256 devices in a mesh: fsdp: 64 (over y_hi, z, x), tp: 4 (over y_lo, core).
Axes of the slice: x: 4, y: 4 (y_hi: 2, y_lo: 2; y = y_hi * 2 + y_lo), z: 8, core: 2. Of those that a mesh axis runs over, the one named last changes fastest.
Arguments:
- latents: bfloat16 [32768, 3072], P(('fsdp', 'tp')), may hold values from -6 to 6
- noise: bfloat16 [32768, 3072], P(('fsdp', 'tp')), may hold values from -6 to 6, as said below
- timestep: int32 [32], replicated, may hold values from 0 to 999
- winner: int32 [32], replicated, may hold values from 0 to 1
- norm_gain: float32 [3072], replicated, may hold values from 0.5 to 1.5
- reference_weight: bfloat16 [3072, 3072], P('tp'), may hold values from -1 to 1
- policy_master: float32 [3072, 3072], P('fsdp', 'tp'), may hold values from -1 to 1
- moment_first: float32 [3072, 3072], P('fsdp', 'tp'), may hold values from -0.06 to 0.06
- moment_second: float32 [3072, 3072], P('fsdp', 'tp'), may hold values from 1e-05 to 0.001
Outputs:
- new_master: float32 [3072, 3072], P('fsdp', 'tp')
- new_first: float32 [3072, 3072], P('fsdp', 'tp')
- new_second: float32 [3072, 3072], P('fsdp', 'tp')
- loss: float32 [], replicated
The draws below stay inside these ranges and needn't reach their ends.
Inputs may be any that keep to these rules, and one draw needn't show every extreme that they name: The two images of a pair have equal noise, row for row.
All inputs are finite; a program needn't handle non-finite values.
Results may differ from the reference program's by a relative error of at most 0.0049.
Values may be sent and summed in bfloat16 or wider, within the bound.
No kernel may reach another device: no remote copies, remote signals or barrier semaphores. Data moves between devices by JAX's collectives and lax.ppermute only.
A program may use at most 128 MiB of HBM per device.

```python
import math
import jax
import jax.numpy as jnp
from jax import lax

D = 3072
STEPS = 1000
ADAM_STEP = 100
SEQ = 512
TOKENS = 32768
NSEQ = 64
PAIRS = 32


def shared_weight(key):
    base = jnp.clip(jax.random.normal(key, (D, D), jnp.float32), -6.0, 6.0)
    return base


def draw_reference_weight(key, part):
    base = shared_weight(key)
    return (base * D ** (-0.5)).astype(jnp.bfloat16)


def draw_policy_master(key, part):
    base = shared_weight(key)
    key = jax.random.fold_in(key, 11)
    change = jnp.clip(jax.random.normal(key, (D, D), jnp.float32), -6.0, 6.0)
    return ((base + 0.2 * change) * D ** (-0.5)).astype(jnp.float32)


def draw_noise(key, part):
    key = jax.random.fold_in(key, 5)
    single = jnp.clip(jax.random.normal(key, (PAIRS, 1, SEQ, D), jnp.float32), -6.0, 6.0)
    return jnp.broadcast_to(single, (PAIRS, 2, SEQ, D)).reshape(TOKENS, D).astype(jnp.bfloat16)


def touch_ends(values, key, low, top_value):
    longest = values.shape.index(max(values.shape))
    spots = []
    for shift in (0, 1):
        where = [jax.random.randint(jax.random.fold_in(key, axis), (), 0, length) for axis, length in enumerate(values.shape)]
        where[longest] = (where[longest] + shift) % values.shape[longest]
        spots.append(tuple(where))
    return values.at[spots[0]].set(low).at[spots[1]].set(top_value)


def block_scale(stream_key, shape, split, smallest, largest):
    loudness, own = 1.0, jax.random.fold_in(stream_key, 6)
    for position, blocks in split:
        heights = jnp.exp(jax.random.uniform(jax.random.fold_in(own, position), (blocks,), jnp.float32, smallest / len(split), largest / len(split)))
        loudness = loudness * jnp.repeat(heights, shape[position] // blocks).reshape([-1 if axis == position else 1 for axis in range(len(shape))])
    return loudness


def centred(stream_key, extent, scale, bound, split=(), held_as=jnp.bfloat16):
    array = scale * jax.random.normal(stream_key, extent, jnp.float32)
    if split:
        array = array * block_scale(stream_key, extent, split, -0.22, 0.18)
    return jnp.clip(array, -bound, bound).astype(held_as)


def setup_inputs(seed: int = 0) -> dict:
    splits = jax.random.split(jax.random.key(seed), 10)
    latents = centred(splits[0], (TOKENS, D), 1.0, 6.0, ((0, 256),))
    noise = draw_noise(jax.random.fold_in(splits[9], 71), 0)
    timestep = touch_ends(jax.random.randint(splits[2], (PAIRS,), 0, STEPS), jax.random.fold_in(splits[2], 1), 0, STEPS - 1).astype(jnp.int32)
    winner = touch_ends(jax.random.randint(splits[3], (PAIRS,), 0, 2), jax.random.fold_in(splits[3], 1), 0, 1).astype(jnp.int32)
    norm_gain = jnp.clip(1.0 + 0.1 * jax.random.normal(splits[4], (D,), jnp.float32), 0.5, 1.5)
    reference_weight = draw_reference_weight(jax.random.fold_in(splits[9], 71), 0)
    policy_master = draw_policy_master(jax.random.fold_in(splits[9], 71), 0)
    moment_first = centred(splits[7], (D, D), 0.01, 0.06, ((0, 64), (1, 4)), jnp.float32)
    moment_second = jnp.clip(jnp.exp(math.log(0.001) - 4.6051703 * jax.random.uniform(splits[8], (D, D), jnp.float32) ** block_scale(splits[8], (D, D), ((0, 64), (1, 4)), -0.2, 0.2)), 9.999999747378752e-06, 0.001)
    return {"latents": latents, "noise": noise, "timestep": timestep, "winner": winner, "norm_gain": norm_gain, "reference_weight": reference_weight, "policy_master": policy_master, "moment_first": moment_first, "moment_second": moment_second}


BETA = 5000.0

def normalize(noisy, gain):
    mean_sq = lax.optimization_barrier(jnp.mean(noisy * noisy, axis=1, keepdims=True))
    return jax.nn.gelu(noisy * lax.rsqrt(mean_sq + 1e-06) * gain, approximate=True).astype(jnp.bfloat16)

def preference(policy_error, reference_error, winner):
    gap = (policy_error - reference_error).reshape(-1, 2)
    first_wins = winner == 0
    gap_win = jnp.where(first_wins, gap[:, 0], gap[:, 1])
    gap_lose = jnp.where(first_wins, gap[:, 1], gap[:, 0])
    margin = -0.5 * BETA * (gap_win - gap_lose)
    loss = jnp.mean(jax.nn.softplus(-margin))
    weight = jax.nn.sigmoid(-margin) * BETA / (2.0 * gap.shape[0])
    first = jnp.where(first_wins, weight, -weight)
    return (loss, jnp.stack([first, -first], axis=1).reshape(-1))

def adam_update(master, first, second, gradient):
    new_first = 0.9 * first + 0.1 * gradient
    new_second = 0.999 * second + 0.001 * gradient * gradient
    first_hat = new_first / (1.0 - 0.9 ** ADAM_STEP)
    second_hat = new_second / (1.0 - 0.999 ** ADAM_STEP)
    new_master = master - 0.001 * (first_hat / (jnp.sqrt(second_hat) + 1e-08) + 0.01 * master)
    return (new_master, new_first, new_second)

def reference(latents, noise, timestep, winner, norm_gain, reference_weight, policy_master, moment_first, moment_second):
    policy_bf = policy_master.astype(jnp.bfloat16)
    seq_times = (timestep.astype(jnp.float32) + 0.5) / STEPS

    def prepare(index):
        start = (index * SEQ).astype(jnp.int32)
        clean = lax.dynamic_slice_in_dim(latents, start, SEQ, 0).astype(jnp.float32)
        drawn = lax.dynamic_slice_in_dim(noise, start, SEQ, 0).astype(jnp.float32)
        moment = seq_times[index // 2]
        noisy = (1.0 - moment) * clean + moment * drawn
        target = drawn - clean
        features = normalize(noisy, norm_gain)
        policy_out = lax.optimization_barrier(jnp.dot(features, policy_bf, preferred_element_type=jnp.float32).astype(jnp.bfloat16)).astype(jnp.float32)
        return (noisy - target, features, policy_out)

    def errors(index):
        base, features, policy_out = prepare(index)
        summed = jnp.dot(features, reference_weight, preferred_element_type=jnp.float32)
        policy_diff = base + policy_out
        ref_diff = base + summed
        return (jnp.sum(policy_diff * policy_diff), jnp.sum(ref_diff * ref_diff))
    indices = jnp.arange(NSEQ, dtype=jnp.int32)
    policy_sq, ref_sq = lax.map(errors, indices)
    scale = float(SEQ * D)
    loss, coefficient = preference(policy_sq / scale, ref_sq / scale, winner)

    def accumulate(total, index):
        base, features, policy_out = prepare(index)
        velocity_grad = (coefficient[index] * (2.0 / scale) * (base + policy_out)).astype(jnp.bfloat16)
        term = lax.dot_general(features, velocity_grad, (((0,), (0,)), ((), ())), preferred_element_type=jnp.float32)
        return (total + term, None)
    gradient, _ = lax.scan(accumulate, jnp.zeros((D, D), jnp.float32), indices)
    new_master, new_first, new_second = adam_update(policy_master, moment_first, moment_second, gradient)
    return (new_master, new_first, new_second, loss)
```

```python
import jax
import jax.numpy as jnp
import numpy as np
from jax import lax
from jax.sharding import Mesh
from jax.sharding import PartitionSpec as P

STEPS = 1000
ADAM_STEP = 100
BETA = 5000.0
AXES = ("yh", "z", "xh", "xl", "yl", "c")
SIZES = (2, 8, 2, 2, 2, 2)
bf16 = jnp.bfloat16
f32 = jnp.float32


def normalize(noisy, gain):
    mean_sq = jnp.mean(noisy * noisy, axis=1, keepdims=True)
    return jax.nn.gelu(noisy * lax.rsqrt(mean_sq + 1e-06) * gain, approximate=True).astype(bf16)


def adam_update(master, first, second, gradient):
    new_first = 0.9 * first + 0.1 * gradient
    new_second = 0.999 * second + 0.001 * gradient * gradient
    first_hat = new_first / (1.0 - 0.9**ADAM_STEP)
    second_hat = new_second / (1.0 - 0.999**ADAM_STEP)
    new_master = master - 0.001 * (first_hat / (jnp.sqrt(second_hat) + 1e-08) + 0.01 * master)
    return (new_master, new_first, new_second)


def flip(x, *axes):
    last = 2 ** len(axes) - 1
    return lax.ppermute(x, axes, [(i, last - i) for i in range(last + 1)])


def ordered(index, own, other):
    return jnp.where(
        index == 0, jnp.concatenate([own, other]), jnp.concatenate([other, own])
    )


def body(
    latents, noise, timestep, winner, norm_gain, reference_weight, policy_master, moment_first, moment_second
):
    tok, width = latents.shape
    yh, z, xh, xl, yl, c = (lax.axis_index(a) for a in AXES)
    half = policy_master.shape[1] // 2
    pair = (yh * SIZES[1] + z) * SIZES[2] + xh
    count_pairs = timestep.shape[0]
    scale = float(4 * tok * width)
    time = (lax.dynamic_index_in_dim(timestep, pair, 0, False).astype(f32) + 0.5) / STEPS
    wins = lax.dynamic_index_in_dim(winner, pair, 0, False) == xl
    sign = jnp.where(wins, 1.0, -1.0).astype(f32)

    def columns(array, dx, dy, dc):
        block = ((yl ^ dy) * 2 + (c ^ dc)) * 2 + (xl ^ dx)
        return lax.dynamic_slice_in_dim(array, block * half, half, 1)

    policy_bf = policy_master.astype(bf16)
    own_w = lax.dynamic_slice_in_dim(policy_bf, xl * half, half, 1)
    other_w = flip(lax.dynamic_slice_in_dim(policy_bf, (1 - xl) * half, half, 1), "xl")
    policy_cols = lax.all_gather(ordered(xl, own_w, other_w), ("yh", "z", "xh"), axis=0, tiled=True)

    clean, drawn = latents.astype(f32), noise.astype(f32)
    feats = normalize((1.0 - time) * clean + time * drawn, norm_gain)
    h = tok // 2
    feats_y, feats_x = flip(feats, "yl"), flip(feats, "xl")
    feats_d = jnp.concatenate([flip(feats_y[:h], "xl"), flip(feats_x[h:], "yl")])
    group_feats = jnp.concatenate(
        [feats, feats_y, flip(feats, "c"), flip(feats_y, "c")]
        + [feats_x, feats_d, flip(feats_x, "c"), flip(feats_d, "c")]
    )

    def pack(dx, dy, dc, with_noise):
        parts = [columns(latents, dx, dy, dc)]
        return parts + ([columns(noise, dx, dy, dc)] if with_noise else [])

    got_y = flip(jnp.stack(pack(0, 1, 0, True) + pack(0, 1, 1, True)), "yl")
    got_x = flip(jnp.stack(pack(1, 0, 0, False) + pack(1, 0, 1, False)), "xl")
    got_d = flip(jnp.stack(pack(1, 1, 0, False) + pack(1, 1, 1, False)), "xl", "yl")
    swap = flip(
        jnp.concatenate([jnp.stack(pack(0, 0, 1, True)), got_y[2:], got_x[1:], got_d[1:]]), "c"
    )
    clean_own = jnp.concatenate([columns(latents, 0, 0, 0), got_y[0], swap[0], swap[2]])
    clean_other = jnp.concatenate([got_x[0], got_d[0], swap[4], swap[5]])
    drawn_cols = jnp.concatenate([columns(noise, 0, 0, 0), got_y[1], swap[1], swap[3]])
    clean_cols = jnp.stack([clean_own, clean_other]).astype(f32)
    drawn_cols = drawn_cols.astype(f32)[None]
    base = ((1.0 - time) * clean_cols + time * drawn_cols) - (drawn_cols - clean_cols)
    base = base.reshape(-1, half)
    signs = jnp.where(jnp.arange(base.shape[0])[:, None] < base.shape[0] // 2, sign, -sign)

    ref_c = flip(columns(reference_weight, 0, 0, 1), "c")
    ref_y = flip(columns(reference_weight, 0, 1, 0), "yh", "yl")
    ref_yc = flip(columns(reference_weight, 0, 1, 1), "yh", "yl", "c")
    ref_cols = ordered(
        yl, ordered(c, columns(reference_weight, 0, 0, 0), ref_c), ordered(c, ref_y, ref_yc)
    )

    policy_out = jnp.dot(group_feats, policy_cols, preferred_element_type=f32).astype(bf16).astype(f32)
    policy_diff = base + policy_out
    grad_cols = (signs * policy_diff).astype(bf16)
    partial = lax.dot_general(
        group_feats, grad_cols, (((0,), (0,)), ((), ())), preferred_element_type=f32
    ).astype(bf16)
    partial = partial.reshape(2, SIZES[1], 2, -1, half)

    def owned_by(dy, dx):
        block = lax.dynamic_index_in_dim(partial, yh ^ dy, 0, False)
        return lax.dynamic_index_in_dim(block, xh ^ dx, 1, False)

    got = [owned_by(0, 0), flip(owned_by(0, 1), "xh"), flip(owned_by(1, 0), "yh"), flip(owned_by(1, 1), "yh", "xh")]

    ref_diff = base + jnp.dot(group_feats, ref_cols, preferred_element_type=f32)
    gap = jnp.sum(signs * (policy_diff * policy_diff - ref_diff * ref_diff))
    gaps = lax.all_gather(gap, ("yh", "xh", "xl", "yl", "c")).reshape(2, 2, -1).sum(axis=2)
    margin = -0.5 * BETA * (gaps / scale)
    loss = jnp.sum(jax.nn.softplus(-margin))
    for step in (1, 2, 4):
        loss = loss + lax.ppermute(loss, "z", [(i, i ^ step) for i in range(SIZES[1])])
    loss = loss / count_pairs
    weight = jax.nn.sigmoid(-margin) * BETA / (2.0 * count_pairs) * (2.0 / scale)

    def weight_of(dy, dx):
        return weight[yh ^ dy, xh ^ dx]

    summed = (
        weight_of(0, 0) * got[0].astype(f32)
        + weight_of(0, 1) * got[1].astype(f32)
        + weight_of(1, 0) * got[2].astype(f32)
        + weight_of(1, 1) * got[3].astype(f32)
    ).astype(bf16)
    rows = policy_master.shape[0]
    blocks = lax.all_to_all(
        summed.reshape(-1, rows, half), ("z", "xl"), split_axis=0, concat_axis=0, tiled=True
    )
    blocks = blocks.reshape(SIZES[1], 2, rows, half).astype(f32).sum(axis=0)
    gradient = jnp.concatenate([blocks[0], blocks[1]], axis=1)
    return adam_update(policy_master, moment_first, moment_second, gradient) + (loss,)


def solution(mesh):
    fine = Mesh(mesh.devices.reshape(SIZES), AXES)
    fsdp, tp = AXES[:4], AXES[4:]
    return jax.shard_map(
        body,
        mesh=fine,
        in_specs=(P(AXES, None), P(AXES, None), P(), P(), P(), P(tp, None))
        + (P(fsdp, tp),) * 3,
        out_specs=(P(fsdp, tp), P(fsdp, tp), P(fsdp, tp), P()),
        check_vma=False,
    )
```

```python
import jax
import jax.numpy as jnp
import numpy as np
from jax import lax
from jax.experimental import pallas as pl
from jax.experimental.pallas import tpu as pltpu
from jax.sharding import Mesh
from jax.sharding import PartitionSpec as P

STEPS = 1000
ADAM_STEP = 100
BETA = 5000.0
AXES = ("yh", "z", "xh", "xl", "yl", "c")
SIZES = (2, 8, 2, 2, 2, 2)
bf16 = jnp.bfloat16
f32 = jnp.float32


def normalize(noisy, gain):
    mean_sq = jnp.mean(noisy * noisy, axis=1, keepdims=True)
    return jax.nn.gelu(noisy * lax.rsqrt(mean_sq + 1e-06) * gain, approximate=True).astype(bf16)


def adam_update(master, first, second, gradient):
    new_first = 0.9 * first + 0.1 * gradient
    new_second = 0.999 * second + 0.001 * gradient * gradient
    first_hat = new_first / (1.0 - 0.9**ADAM_STEP)
    second_hat = new_second / (1.0 - 0.999**ADAM_STEP)
    new_master = master - 0.001 * (first_hat / (jnp.sqrt(second_hat) + 1e-08) + 0.01 * master)
    return (new_master, new_first, new_second)


def flip(x, *axes):
    last = 2 ** len(axes) - 1
    return lax.ppermute(x, axes, [(i, last - i) for i in range(last + 1)])


def shift(x, step):
    return lax.ppermute(x, "z", [(i, (i + step) % SIZES[1]) for i in range(SIZES[1])])


def after(x, *others):
    return lax.optimization_barrier((x,) + others)[0]


def ordered(index, own, other):
    return jnp.where(
        index == 0, jnp.concatenate([own, other]), jnp.concatenate([other, own])
    )


def pack_kernel(half, at, timestep, latents, noise, gain, feats, send_y, send_x, send_c):
    time = (timestep[at[0]].astype(f32) + 0.5) / STEPS
    clean, drawn = latents[...].astype(f32), noise[...].astype(f32)
    value = normalize((1.0 - time) * clean + time * drawn, gain[...])
    width = value.shape[1]
    low, high = value[:, : width // 2], value[:, width // 2 :]
    value = jnp.where(at[1] == 0, value, jnp.concatenate([high, low], 1))

    def fill(out, places, after_feats):
        col = 0
        for array, place in places:
            start = pl.multiple_of(at[place] * half, 128)
            out[:, col : col + half] = array[:, pl.ds(start, half)]
            col += half
        out[:, col : col + width] = value
        col += width
        for array, place in after_feats:
            start = pl.multiple_of(at[place] * half, 128)
            out[:, col : col + half] = array[:, pl.ds(start, half)]
            col += half

    diagonal = [(latents, 8), (latents, 7)]
    feats[...] = value
    fill(send_y, [(latents, 3), (noise, 3), (latents, 4), (noise, 4)], diagonal)
    fill(send_x, [(latents, 5), (latents, 6)], diagonal)
    fill(send_c, [(latents, 2), (noise, 2)], [])


def pack(at, timestep, latents, noise, gain, half):
    tok, width = latents.shape
    rows = tok // 4
    widths = (width, width + 6 * half, width + 4 * half, width + 2 * half)
    small = pl.BlockSpec(memory_space=pltpu.SMEM)
    return pl.pallas_call(
        lambda *refs: pack_kernel(half, *refs),
        grid=(tok // rows,),
        in_specs=[
            small,
            small,
            pl.BlockSpec((rows, width), lambda i: (i, 0)),
            pl.BlockSpec((rows, width), lambda i: (i, 0)),
            pl.BlockSpec((1, width), lambda i: (0, 0)),
        ],
        out_specs=[pl.BlockSpec((rows, w), lambda i: (i, 0)) for w in widths],
        out_shape=[jax.ShapeDtypeStruct((tok, w), bf16) for w in widths],
        compiler_params=pltpu.CompilerParams(vmem_limit_bytes=16 * 2**20),
        cost_estimate=pl.CostEstimate(
            flops=20 * tok * width, bytes_accessed=15 * tok * width, transcendentals=tok * width
        ),
        name="pack",
    )(at, timestep, latents, noise, gain[None])


def project_kernel(
    half, at, timestep, winner, latents, noise, feats, got_y, got_c, got_yc, got_x, diag_0, diag_1,
    got_xc, diag_c0, diag_c1, policy, reference, ref_y, ref_c, gap, near, near_x, far, far_x,
    rows_ref, both, clean, drawn, grad, sems,
):
    tok, width = feats.shape
    h = tok // 2
    pair, yh, yl, c, xh, xl, own = (at[i] for i in range(7))
    time = (timestep[pair].astype(f32) + 0.5) / STEPS
    sign = jnp.where(winner[pair] == xl, 1.0, -1.0).astype(f32)
    mine = pl.ds(pl.multiple_of(own * half, 128), half)
    count = [0]

    def start(source, target):
        copy = pltpu.make_async_copy(source, target, sems.at[count[0]])
        count[0] += 1
        copy.start()
        return copy

    def lanes(first, size=half):
        return pl.ds(first * half, size)

    def rows_of(k):
        return pl.ds(k * tok, tok)

    n_z, depth = policy.shape[0], policy.shape[2]
    weight_copies = [
        start(policy.at[z, y], both.at[pl.ds((y * n_z + z) * depth, depth), lanes(0)])
        for z in range(n_z)
        for y in range(2)
    ]
    block = reference.shape[0]
    for dy, dc, source in (
        (0, 0, reference.at[:, mine]),
        (0, 1, ref_c.at[:, lanes(0)]),
        (1, 0, ref_y.at[:, lanes(0)]),
        (1, 1, ref_c.at[:, lanes(1)]),
    ):
        place = ((yl ^ dy ^ yh) * 2 + (c ^ dc)) * block
        target = both.at[pl.ds(pl.multiple_of(place, block), block), lanes(1)]
        weight_copies.append(start(source, target))

    def piece(k, source, feats_at, clean_at, drawn_at):
        copies = [
            start(source.at[:, lanes(feats_at, width)], rows_ref.at[rows_of(k)]),
            start(source.at[:, lanes(clean_at)], clean.at[rows_of(k)]),
        ]
        if drawn_at is not None:
            copies.append(start(source.at[:, lanes(drawn_at)], drawn.at[rows_of(k)]))
        return copies

    def halves(k, source):
        copies = []
        for i in range(2):
            part, rows = source[i], pl.ds(k * tok + i * h, h)
            copies.append(start(part.at[:, lanes(0, width)], rows_ref.at[rows]))
            copies.append(start(part.at[:, lanes(9 if k == 5 else 8)], clean.at[rows]))
        return copies

    chunks = [
        [
            start(feats, rows_ref.at[rows_of(0)]),
            start(latents.at[:, mine], clean.at[rows_of(0)]),
            start(noise.at[:, mine], drawn.at[rows_of(0)]),
        ]
        + piece(1, got_y, 4, 0, 1),
        piece(2, got_c, 2, 0, 1) + piece(3, got_yc, 4, 2, 3),
        piece(4, got_x, 2, 0, None) + halves(5, (diag_0, diag_1)),
        piece(6, got_xc, 2, 1, None) + halves(7, (diag_c0, diag_c1)),
    ]
    for copy in weight_copies:
        copy.wait()
    total = jnp.zeros((1, half), f32)
    for i, copies in enumerate(chunks):
        for copy in copies:
            copy.wait()
        rows = pl.ds(i * 2 * tok, 2 * tok)
        out = jnp.dot(rows_ref[rows, :], both[...], preferred_element_type=f32)
        start_rows = clean[rows, :].astype(f32)
        noise_rows = drawn[pl.ds((i % 2) * 2 * tok, 2 * tok), :].astype(f32)
        base = ((1.0 - time) * start_rows + time * noise_rows) - (noise_rows - start_rows)
        policy_diff = base + out[:, :half].astype(bf16).astype(f32)
        ref_diff = base + out[:, half:]
        signed = sign if i < 2 else -sign
        grad[rows, :] = (signed * policy_diff).astype(bf16)
        excess = policy_diff * policy_diff - ref_diff * ref_diff
        total = total + signed * jnp.sum(excess, axis=0, keepdims=True)
    gap[...] = jnp.broadcast_to(jnp.sum(total, axis=1, keepdims=True), gap.shape)

    per = depth // 2
    for y, same, other in ((1, far, far_x), (0, near, near_x)):
        for z in range(0, n_z, 2):
            part = lax.dot_general(
                rows_ref[:, pl.ds((y * n_z + z) * depth, 2 * depth)],
                grad[...],
                (((0,), (0,)), ((), ())),
                preferred_element_type=f32,
            ).astype(bf16)
            for k in range(2):
                low = part[2 * k * per : (2 * k + 1) * per]
                high = part[(2 * k + 1) * per : (2 * k + 2) * per]
                rows = pl.ds((z + k) * per, per)
                same[rows, :] = jnp.where(xh == 0, low, high)
                other[rows, :] = jnp.where(xh == 0, high, low)
    tail = pl.ds(n_z * per, 16)
    for out in (near, near_x, far, far_x):
        out[tail, :] = jnp.zeros((16, half), bf16)


def project(at, timestep, winner, half, *arrays):
    tok, width = arrays[2].shape
    policy = arrays[12]
    out_rows = policy.shape[0] * policy.shape[2] // 2 + 16
    small = pl.BlockSpec(memory_space=pltpu.SMEM)
    block = jax.ShapeDtypeStruct((out_rows, half), bf16)
    return pl.pallas_call(
        lambda *refs: project_kernel(half, *refs),
        in_specs=[small] * 3 + [pl.BlockSpec(memory_space=pl.ANY)] * len(arrays),
        out_specs=[pl.BlockSpec(memory_space=pltpu.VMEM)] * 5,
        out_shape=[jax.ShapeDtypeStruct((8, 128), f32)] + [block] * 4,
        scratch_shapes=[
            pltpu.VMEM((8 * tok, width), bf16),
            pltpu.VMEM((width, 2 * half), bf16),
            pltpu.VMEM((8 * tok, half), bf16),
            pltpu.VMEM((4 * tok, half), bf16),
            pltpu.VMEM((8 * tok, half), bf16),
            pltpu.SemaphoreType.DMA((48,)),
        ],
        compiler_params=pltpu.CompilerParams(vmem_limit_bytes=40 * 2**20),
        cost_estimate=pl.CostEstimate(
            flops=6 * 8 * tok * width * half, bytes_accessed=16 * 2**20, transcendentals=0
        ),
        name="project",
    )(at, timestep, winner, *arrays)


def body(
    latents, noise, timestep, winner, norm_gain, reference_weight, policy_master, moment_first, moment_second
):
    tok, width = latents.shape
    yh, z, xh, xl, yl, c = (lax.axis_index(a) for a in AXES)
    half = policy_master.shape[1] // 2
    pair = (yh * SIZES[1] + z) * SIZES[2] + xh
    count_pairs = timestep.shape[0]
    scale = float(4 * tok * width)
    def columns(array, dx, dy, dc):
        block = ((yl ^ dy) * 2 + (c ^ dc)) * 2 + (xl ^ dx)
        return lax.dynamic_slice_in_dim(array, block * half, half, 1)

    policy_bf = policy_master.astype(bf16)
    own_w = lax.dynamic_slice_in_dim(policy_bf, xl * half, half, 1)
    other_w = flip(lax.dynamic_slice_in_dim(policy_bf, (1 - xl) * half, half, 1), "xl")
    own_w = ordered(xl, own_w, other_w)
    same_z = jnp.stack(
        [
            ordered(xh, own_w[None], flip(own_w, "xh")[None]),
            ordered(xh, flip(own_w, "yh")[None], flip(own_w, "yh", "xh")[None]),
        ]
    )[:, None]

    blocks = [
        ((yl ^ dy) * 2 + (c ^ dc)) * 2 + (xl ^ dx)
        for dx, dy in ((0, 0), (0, 1), (1, 0), (1, 1))
        for dc in (0, 1)
    ]
    at = jnp.stack([pair, yh] + blocks[1:])
    feats, send_y, send_x, send_c = pack(at, timestep, latents, noise, norm_gain, half)
    send_y, send_x, send_c, weight_in, _ = lax.optimization_barrier(
        (send_y, send_x, send_c, reference_weight, same_z)
    )
    got_y, got_x, got_c = flip(send_y, "yl"), flip(send_x, "xl"), flip(send_c, "c")

    ref_y = flip(
        jnp.concatenate([columns(weight_in, 0, 1, 0), columns(weight_in, 0, 1, 1)], 1), "yh", "yl"
    )
    ref_c = flip(jnp.concatenate([columns(weight_in, 0, 0, 1), ref_y[:, half:]], 1), "c")
    n_z = SIZES[1]
    per_z = lax.all_gather(same_z.reshape(-1, half), "z").reshape(n_z, 2, -1, half)

    h = tok // 2
    diag = [flip(got_y[:h, 4 * half :], "xl"), flip(got_x[h:, 2 * half :], "yl")]
    diag_c = [flip(part, "c") for part in diag]
    got_yc, got_xc = flip(got_y, "c"), flip(got_x, "c")

    places = jnp.stack([pair, yh, yl, c, xh, xl, blocks[0]])
    gap, near, near_x, far, far_x = project(
        places, timestep, winner, half, latents, noise, feats, got_y, got_c, got_yc, got_x,
        *diag, got_xc, *diag_c, per_z, reference_weight, ref_y, ref_c,
    )

    gap = gap[:1, :1]
    gap = gap + flip(gap, "c")
    gap = flip(gap, "xl") + flip(gap, "yl") + (flip(gap, "xl", "yl") + gap)
    margin = -0.5 * BETA * (gap / scale)
    first = lax.reduce_precision(margin, 8, 7)
    second = lax.reduce_precision(margin - first, 8, 7)
    terms = jnp.concatenate([first, second, (margin - first) - second]).astype(bf16)
    terms = jnp.broadcast_to(jnp.concatenate([terms, jnp.zeros((13, 1), bf16)]), (16, half))
    size = near.shape[0] - 16

    def with_margin(block):
        return lax.dynamic_update_slice(block, terms, (size, 0))

    got = [
        near,
        flip(with_margin(near_x), "xh"),
        flip(with_margin(far), "yh"),
        flip(with_margin(far_x), "yh", "xh"),
    ]

    def margin_of(block):
        first, second, third = (block[size + i : size + i + 1, :1].astype(f32) for i in range(3))
        return (first + second) + third

    margins = [margin] + [margin_of(g) for g in got[1:]]
    weights = [
        jax.nn.sigmoid(-m) * BETA / (2.0 * count_pairs) * (2.0 / scale) for m in margins
    ]
    losses = [jax.nn.softplus(-m) for m in margins]
    loss = ((losses[0] + losses[1]) + (losses[2] + losses[3])).reshape(())
    for step in (1, 2, 4):
        loss = loss + lax.ppermute(loss, "z", [(i, i ^ step) for i in range(n_z)])
    loss = loss / count_pairs
    got = [g[:size] for g in got]

    summed = sum(w * g.astype(f32) for w, g in zip(weights, got)).astype(bf16)
    rows = policy_master.shape[0]
    blocks = lax.all_to_all(
        summed.reshape(-1, rows, half), ("z", "xl"), split_axis=0, concat_axis=0, tiled=True
    )
    blocks = blocks.reshape(SIZES[1], 2, rows, half).astype(f32).sum(axis=0)
    gradient = jnp.concatenate([blocks[0], blocks[1]], axis=1)
    return adam_update(policy_master, moment_first, moment_second, gradient) + (loss,)


def solution(mesh):
    fine = Mesh(mesh.devices.reshape(SIZES), AXES)
    fsdp, tp = AXES[:4], AXES[4:]
    return jax.shard_map(
        body,
        mesh=fine,
        in_specs=(P(AXES, None), P(AXES, None), P(), P(), P(), P(tp, None))
        + (P(fsdp, tp),) * 3,
        out_specs=(P(fsdp, tp), P(fsdp, tp), P(fsdp, tp), P()),
        check_vma=False,
    )
```

```python
import jax
import jax.numpy as jnp
import numpy as np
from jax import lax
from jax.experimental import pallas as pl
from jax.experimental.pallas import tpu as pltpu
from jax.sharding import Mesh
from jax.sharding import PartitionSpec as P

STEPS = 1000
ADAM_STEP = 100
BETA = 5000.0
AXES = ("yh", "z", "xh", "xl", "yl", "c")
SIZES = (2, 8, 2, 2, 2, 2)
bf16 = jnp.bfloat16
f32 = jnp.float32


def normalize(noisy, gain):
    mean_sq = jnp.mean(noisy * noisy, axis=1, keepdims=True)
    return jax.nn.gelu(noisy * lax.rsqrt(mean_sq + 1e-06) * gain, approximate=True).astype(bf16)


def adam_update(master, first, second, gradient):
    new_first = 0.9 * first + 0.1 * gradient
    new_second = 0.999 * second + 0.001 * gradient * gradient
    first_hat = new_first / (1.0 - 0.9**ADAM_STEP)
    second_hat = new_second / (1.0 - 0.999**ADAM_STEP)
    new_master = master - 0.001 * (first_hat / (jnp.sqrt(second_hat) + 1e-08) + 0.01 * master)
    return (new_master, new_first, new_second)


def flip(x, *axes):
    last = 2 ** len(axes) - 1
    return lax.ppermute(x, axes, [(i, last - i) for i in range(last + 1)])


def shift(x, step):
    return lax.ppermute(x, "z", [(i, (i + step) % SIZES[1]) for i in range(SIZES[1])])


def after(x, *others):
    return lax.optimization_barrier((x,) + others)[0]


def ordered(index, own, other):
    return jnp.where(
        index == 0, jnp.concatenate([own, other]), jnp.concatenate([other, own])
    )


def pack_kernel(half, at, timestep, latents, noise, gain, feats, send, send_y, send_x, send_c):
    time = (timestep[at[0]].astype(f32) + 0.5) / STEPS
    clean, drawn = latents[...].astype(f32), noise[...].astype(f32)
    value = normalize((1.0 - time) * clean + time * drawn, gain[...])
    width = value.shape[1]
    low, high = value[:, : width // 2], value[:, width // 2 :]
    value = jnp.where(at[1] == 0, value, jnp.concatenate([high, low], 1))

    def fill(out, places, feats_at=None):
        for col, (array, place) in enumerate(places):
            start = pl.multiple_of(at[place] * half, 128)
            col = col * half + (width if feats_at == 0 else 0)
            out[:, col : col + half] = array[:, pl.ds(start, half)]
        if feats_at is not None:
            out[:, feats_at * half : feats_at * half + width] = value

    feats[...] = value
    fill(send, [(latents, 8), (latents, 7)], 0)
    fill(send_y, [(latents, 3), (noise, 3), (latents, 4), (noise, 4)])
    fill(send_x, [(latents, 5), (latents, 6)])
    fill(send_c, [(latents, 2), (noise, 2)], 2)


def pack(at, timestep, latents, noise, gain, half):
    tok, width = latents.shape
    rows = tok // 4
    widths = (width, width + 2 * half, 4 * half, 2 * half, width + 2 * half)
    small = pl.BlockSpec(memory_space=pltpu.SMEM)
    return pl.pallas_call(
        lambda *refs: pack_kernel(half, *refs),
        grid=(tok // rows,),
        in_specs=[
            small,
            small,
            pl.BlockSpec((rows, width), lambda i: (i, 0)),
            pl.BlockSpec((rows, width), lambda i: (i, 0)),
            pl.BlockSpec((1, width), lambda i: (0, 0)),
        ],
        out_specs=[pl.BlockSpec((rows, w), lambda i: (i, 0)) for w in widths],
        out_shape=[jax.ShapeDtypeStruct((tok, w), bf16) for w in widths],
        compiler_params=pltpu.CompilerParams(vmem_limit_bytes=56 * 2**20),
        cost_estimate=pl.CostEstimate(
            flops=20 * tok * width, bytes_accessed=15 * tok * width, transcendentals=tok * width
        ),
        name="pack",
    )(at, timestep, latents, noise, gain[None])


def project_kernel(
    half, at, timestep, winner, latents, noise, feats, rows_y, rows_yc, rows_x, rows_xc, got_c,
    got_y, got_yc, got_x, got_xc, diag_0, diag_1, diag_c0, diag_c1, policy, reference, ref_y, ref_c,
    gap, near, near_x, far, far_x,
    rows_ref, both, clean, drawn, grad, sems,
):
    tok, width = feats.shape
    h = tok // 2
    pair, yh, yl, c, xh, xl, own = (at[i] for i in range(7))
    time = (timestep[pair].astype(f32) + 0.5) / STEPS
    sign = jnp.where(winner[pair] == xl, 1.0, -1.0).astype(f32)
    mine = pl.ds(pl.multiple_of(own * half, 128), half)
    count = [0]

    def start(source, target):
        copy = pltpu.make_async_copy(source, target, sems.at[count[0]])
        count[0] += 1
        copy.start()
        return copy

    def lanes(first, size=half):
        return pl.ds(first * half, size)

    def rows_of(k):
        return pl.ds(k * tok, tok)

    n_z, depth = policy.shape[0], policy.shape[2]
    weight_copies = [
        start(policy.at[z, y], both.at[pl.ds((y * n_z + z) * depth, depth), lanes(0)])
        for z in range(n_z)
        for y in range(2)
    ]
    block = reference.shape[0]
    for dy, dc, source in (
        (0, 0, reference.at[:, mine]),
        (0, 1, ref_c.at[:, lanes(0)]),
        (1, 0, ref_y.at[:, lanes(0)]),
        (1, 1, ref_c.at[:, lanes(1)]),
    ):
        place = ((yl ^ dy ^ yh) * 2 + (c ^ dc)) * block
        target = both.at[pl.ds(pl.multiple_of(place, block), block), lanes(1)]
        weight_copies.append(start(source, target))

    def piece(k, source, feats_at, beside, clean_at, drawn_at):
        copies = [
            start(source.at[:, lanes(feats_at, width)], rows_ref.at[rows_of(k)]),
            start(beside.at[:, lanes(clean_at)], clean.at[rows_of(k)]),
        ]
        if drawn_at is not None:
            copies.append(start(beside.at[:, lanes(drawn_at)], drawn.at[rows_of(k)]))
        return copies

    def halves(k, source):
        copies = []
        for i in range(2):
            part, rows = source[i], pl.ds(k * tok + i * h, h)
            copies.append(start(part.at[:, lanes(0, width)], rows_ref.at[rows]))
            copies.append(start(part.at[:, lanes(9 if k == 5 else 8)], clean.at[rows]))
        return copies

    chunks = [
        [
            start(feats, rows_ref.at[rows_of(0)]),
            start(latents.at[:, mine], clean.at[rows_of(0)]),
            start(noise.at[:, mine], drawn.at[rows_of(0)]),
        ]
        + piece(1, rows_y, 0, got_y, 0, 1),
        piece(2, got_c, 2, got_c, 0, 1) + piece(3, rows_yc, 0, got_yc, 2, 3),
        piece(4, rows_x, 0, got_x, 0, None) + halves(5, (diag_0, diag_1)),
        piece(6, rows_xc, 0, got_xc, 1, None) + halves(7, (diag_c0, diag_c1)),
    ]
    for copy in weight_copies:
        copy.wait()
    total = jnp.zeros((1, half), f32)
    for i, copies in enumerate(chunks):
        for copy in copies:
            copy.wait()
        rows = pl.ds(i * 2 * tok, 2 * tok)
        out = jnp.dot(rows_ref[rows, :], both[...], preferred_element_type=f32)
        start_rows = clean[rows, :].astype(f32)
        noise_rows = drawn[pl.ds((i % 2) * 2 * tok, 2 * tok), :].astype(f32)
        base = ((1.0 - time) * start_rows + time * noise_rows) - (noise_rows - start_rows)
        policy_diff = base + out[:, :half].astype(bf16).astype(f32)
        ref_diff = base + out[:, half:]
        signed = sign if i < 2 else -sign
        grad[rows, :] = (signed * policy_diff).astype(bf16)
        excess = policy_diff * policy_diff - ref_diff * ref_diff
        total = total + signed * jnp.sum(excess, axis=0, keepdims=True)
    gap[...] = jnp.broadcast_to(jnp.sum(total, axis=1, keepdims=True), gap.shape)

    per = depth // 2
    for y, same, other in ((1, far, far_x), (0, near, near_x)):
        for z in range(0, n_z, 2):
            part = lax.dot_general(
                rows_ref[:, pl.ds((y * n_z + z) * depth, 2 * depth)],
                grad[...],
                (((0,), (0,)), ((), ())),
                preferred_element_type=f32,
            ).astype(bf16)
            for k in range(2):
                low = part[2 * k * per : (2 * k + 1) * per]
                high = part[(2 * k + 1) * per : (2 * k + 2) * per]
                rows = pl.ds((z + k) * per, per)
                same[rows, :] = jnp.where(xh == 0, low, high)
                other[rows, :] = jnp.where(xh == 0, high, low)
    tail = pl.ds(n_z * per, 16)
    for out in (near, near_x, far, far_x):
        out[tail, :] = jnp.zeros((16, half), bf16)


def project(at, timestep, winner, half, *arrays):
    tok, width = arrays[2].shape
    policy = arrays[16]
    out_rows = policy.shape[0] * policy.shape[2] // 2 + 16
    small = pl.BlockSpec(memory_space=pltpu.SMEM)
    block = jax.ShapeDtypeStruct((out_rows, half), bf16)
    return pl.pallas_call(
        lambda *refs: project_kernel(half, *refs),
        in_specs=[small] * 3 + [pl.BlockSpec(memory_space=pl.ANY)] * len(arrays),
        out_specs=[pl.BlockSpec(memory_space=pltpu.VMEM)] * 5,
        out_shape=[jax.ShapeDtypeStruct((8, 128), f32)] + [block] * 4,
        scratch_shapes=[
            pltpu.VMEM((8 * tok, width), bf16),
            pltpu.VMEM((width, 2 * half), bf16),
            pltpu.VMEM((8 * tok, half), bf16),
            pltpu.VMEM((4 * tok, half), bf16),
            pltpu.VMEM((8 * tok, half), bf16),
            pltpu.SemaphoreType.DMA((48,)),
        ],
        compiler_params=pltpu.CompilerParams(vmem_limit_bytes=56 * 2**20),
        cost_estimate=pl.CostEstimate(
            flops=6 * 8 * tok * width * half, bytes_accessed=16 * 2**20, transcendentals=0
        ),
        name="project",
    )(at, timestep, winner, *arrays)


def stamp_kernel(scale, gap, gap_x, gap_y, gap_d, margin, terms):
    total = gap_x[...] + gap_y[...] + (gap_d[...] + gap[...])
    value = -0.5 * BETA * (total / scale)
    margin[...] = value
    value = value[:1, :1]
    first = value.astype(bf16).astype(f32)
    second = (value - first).astype(bf16).astype(f32)
    third = (value - first) - second
    row = lax.broadcasted_iota(jnp.int32, terms.shape, 0)
    rest = jnp.where(row == 2, third, 0.0)
    terms[...] = jnp.where(row == 0, first, jnp.where(row == 1, second, rest)).astype(bf16)


def stamp(scale, half, *gaps):
    return pl.pallas_call(
        lambda *refs: stamp_kernel(scale, *refs),
        out_shape=[
            jax.ShapeDtypeStruct(gaps[0].shape, f32),
            jax.ShapeDtypeStruct((16, half), bf16),
        ],
        name="stamp",
    )(*gaps)


def combine_kernel(factor, margin, near, got_x, got_y, got_d, out):
    size = out.shape[0]

    def weight(value):
        return (jax.nn.sigmoid(-value) * factor)[:1, :1]

    total = weight(margin[...]) * near[:size, :].astype(f32)
    for block in (got_x, got_y, got_d):
        terms = block[size : size + 16, :128].astype(f32)
        value = (terms[0:1] + terms[1:2]) + terms[2:3]
        total = total + weight(value) * block[:size, :].astype(f32)
    out[...] = total.astype(bf16)


def combine(factor, margin, *blocks):
    rows, half = blocks[0].shape
    return pl.pallas_call(
        lambda *refs: combine_kernel(factor, *refs),
        out_shape=jax.ShapeDtypeStruct((rows - 16, half), bf16),
        compiler_params=pltpu.CompilerParams(vmem_limit_bytes=24 * 2**20),
        name="combine",
    )(margin, *blocks)


def body(
    latents, noise, timestep, winner, norm_gain, reference_weight, policy_master, moment_first, moment_second
):
    tok, width = latents.shape
    yh, z, xh, xl, yl, c = (lax.axis_index(a) for a in AXES)
    half = policy_master.shape[1] // 2
    pair = (yh * SIZES[1] + z) * SIZES[2] + xh
    count_pairs = timestep.shape[0]
    scale = float(4 * tok * width)
    def columns(array, dx, dy, dc):
        block = ((yl ^ dy) * 2 + (c ^ dc)) * 2 + (xl ^ dx)
        return lax.dynamic_slice_in_dim(array, block * half, half, 1)

    policy_bf = policy_master.astype(bf16)
    own_w = lax.dynamic_slice_in_dim(policy_bf, xl * half, half, 1)
    other_w = flip(lax.dynamic_slice_in_dim(policy_bf, (1 - xl) * half, half, 1), "xl")
    blocks = [
        ((yl ^ dy) * 2 + (c ^ dc)) * 2 + (xl ^ dx)
        for dx, dy in ((0, 0), (0, 1), (1, 0), (1, 1))
        for dc in (0, 1)
    ]
    at = jnp.stack([pair, yh] + blocks[1:])
    feats, send, send_y, send_x, send_c = pack(at, timestep, latents, noise, norm_gain, half)
    own_w = ordered(xl, own_w, other_w)
    same_z = jnp.stack(
        [
            ordered(xh, own_w[None], after(flip(own_w, "xh"), feats)[None]),
            ordered(xh, flip(own_w, "yh")[None], flip(own_w, "yh", "xh")[None]),
        ]
    )[:, None]

    send, send_c, weight_in, _ = lax.optimization_barrier((send, send_c, reference_weight, same_z))
    rows_y, rows_x, got_c = flip(send, "yl"), flip(send, "xl"), flip(send_c, "c")
    send_y, send_x, rows_y, rows_x = lax.optimization_barrier((send_y, send_x, rows_y, rows_x))
    got_y, got_x = flip(send_y, "yl"), flip(send_x, "xl")

    ref_y = flip(
        jnp.concatenate([columns(weight_in, 0, 1, 0), columns(weight_in, 0, 1, 1)], 1), "yh", "yl"
    )
    ref_y = after(ref_y, got_y)
    ref_c = flip(jnp.concatenate([columns(weight_in, 0, 0, 1), ref_y[:, half:]], 1), "c")

    n_z = SIZES[1]
    per_z = lax.all_gather(same_z.reshape(-1, half), "z").reshape(n_z, 2, -1, half)

    h = tok // 2
    diag = [flip(rows_y[:h], "xl"), flip(rows_x[h:], "yl")]
    diag_c = [flip(part, "c") for part in diag]
    rows_yc, rows_xc = flip(rows_y, "c"), flip(rows_x, "c")
    got_yc, got_xc = flip(got_y, "c"), flip(got_x, "c")

    places = jnp.stack([pair, yh, yl, c, xh, xl, blocks[0]])
    gap, near, near_x, far, far_x = project(
        places, timestep, winner, half, latents, noise, feats, rows_y, rows_yc, rows_x, rows_xc,
        got_c, got_y, got_yc, got_x, got_xc, *diag, *diag_c, per_z, reference_weight, ref_y, ref_c,
    )

    gap = gap + flip(gap, "c")
    margin, terms = stamp(
        scale, half, gap, flip(gap, "xl"), flip(gap, "yl"), flip(gap, "xl", "yl")
    )
    size = near.shape[0] - 16

    def with_margin(block):
        return lax.dynamic_update_slice(block, terms, (size, 0))

    got_x = flip(with_margin(near_x), "xh")
    got_y = flip(with_margin(far), "yh")
    got_d = flip(with_margin(far_x), "yh", "xh")
    loss = jax.nn.softplus(-margin[0, 0])
    for step in (1, 2, 4):
        loss = loss + lax.ppermute(loss, "z", [(i, i ^ step) for i in range(n_z)])
    factor = BETA / (2.0 * count_pairs) * (2.0 / scale)
    summed = combine(factor, after(margin, loss), near, got_x, got_y, got_d)
    loss = after(loss, summed)
    loss = (loss + flip(loss, "xh")) + (flip(loss, "yh") + flip(loss, "yh", "xh"))
    loss = loss / count_pairs
    rows = policy_master.shape[0]
    blocks = lax.all_to_all(
        summed.reshape(-1, rows, half), ("z", "xl"), split_axis=0, concat_axis=0, tiled=True
    )
    blocks = blocks.reshape(SIZES[1], 2, rows, half).astype(f32).sum(axis=0)
    gradient = jnp.concatenate([blocks[0], blocks[1]], axis=1)
    return adam_update(policy_master, moment_first, moment_second, gradient) + (loss,)


def solution(mesh):
    fine = Mesh(mesh.devices.reshape(SIZES), AXES)
    fsdp, tp = AXES[:4], AXES[4:]
    return jax.shard_map(
        body,
        mesh=fine,
        in_specs=(P(AXES, None), P(AXES, None), P(), P(), P(), P(tp, None))
        + (P(fsdp, tp),) * 3,
        out_specs=(P(fsdp, tp), P(fsdp, tp), P(fsdp, tp), P()),
        check_vma=False,
    )
```

```python
import jax
import jax.numpy as jnp
import numpy as np
from jax import lax
from jax.experimental import pallas as pl
from jax.experimental.pallas import tpu as pltpu
from jax.sharding import Mesh
from jax.sharding import PartitionSpec as P

STEPS = 1000
ADAM_STEP = 100
BETA = 5000.0
AXES = ("yh", "z", "xh", "xl", "yl", "c")
SIZES = (2, 8, 2, 2, 2, 2)
bf16 = jnp.bfloat16
f32 = jnp.float32


def normalize(noisy, gain):
    mean_sq = jnp.mean(noisy * noisy, axis=1, keepdims=True)
    return jax.nn.gelu(noisy * lax.rsqrt(mean_sq + 1e-06) * gain, approximate=True).astype(bf16)


def adam_update(master, first, second, gradient):
    new_first = 0.9 * first + 0.1 * gradient
    new_second = 0.999 * second + 0.001 * gradient * gradient
    first_hat = new_first / (1.0 - 0.9**ADAM_STEP)
    second_hat = new_second / (1.0 - 0.999**ADAM_STEP)
    new_master = master - 0.001 * (first_hat / (jnp.sqrt(second_hat) + 1e-08) + 0.01 * master)
    return (new_master, new_first, new_second)


def flip(x, *axes):
    last = 2 ** len(axes) - 1
    return lax.ppermute(x, axes, [(i, last - i) for i in range(last + 1)])


def shift(x, step):
    return lax.ppermute(x, "z", [(i, (i + step) % SIZES[1]) for i in range(SIZES[1])])


def after(x, *others):
    return lax.optimization_barrier((x,) + others)[0]


def ordered(index, own, other):
    return jnp.where(
        index == 0, jnp.concatenate([own, other]), jnp.concatenate([other, own])
    )


def pack_kernel(half, at, timestep, latents, noise, gain, feats, send, send_y, send_x, send_c):
    time = (timestep[at[0]].astype(f32) + 0.5) / STEPS
    clean, drawn = latents[...].astype(f32), noise[...].astype(f32)
    value = normalize((1.0 - time) * clean + time * drawn, gain[...])
    width = value.shape[1]
    low, high = value[:, : width // 2], value[:, width // 2 :]
    value = jnp.where(at[1] == 0, value, jnp.concatenate([high, low], 1))

    def fill(out, places, feats_at=None):
        for col, (array, place) in enumerate(places):
            start = pl.multiple_of(at[place] * half, 128)
            col = col * half + (width if feats_at == 0 else 0)
            out[:, col : col + half] = array[:, pl.ds(start, half)]
        if feats_at is not None:
            out[:, feats_at * half : feats_at * half + width] = value

    feats[...] = value
    fill(send, [(latents, 8), (latents, 7)], 0)
    fill(send_y, [(latents, 3), (noise, 3), (latents, 4), (noise, 4)])
    fill(send_x, [(latents, 5), (latents, 6)])
    fill(send_c, [(latents, 2), (noise, 2)], 2)


def pack(at, timestep, latents, noise, gain, half):
    tok, width = latents.shape
    rows = tok // 4
    widths = (width, width + 2 * half, 4 * half, 2 * half, width + 2 * half)
    small = pl.BlockSpec(memory_space=pltpu.SMEM)
    return pl.pallas_call(
        lambda *refs: pack_kernel(half, *refs),
        grid=(tok // rows,),
        in_specs=[
            small,
            small,
            pl.BlockSpec((rows, width), lambda i: (i, 0)),
            pl.BlockSpec((rows, width), lambda i: (i, 0)),
            pl.BlockSpec((1, width), lambda i: (0, 0)),
        ],
        out_specs=[pl.BlockSpec((rows, w), lambda i: (i, 0)) for w in widths],
        out_shape=[jax.ShapeDtypeStruct((tok, w), bf16) for w in widths],
        compiler_params=pltpu.CompilerParams(vmem_limit_bytes=56 * 2**20),
        cost_estimate=pl.CostEstimate(
            flops=20 * tok * width, bytes_accessed=15 * tok * width, transcendentals=tok * width
        ),
        name="pack",
    )(at, timestep, latents, noise, gain[None])


def project_kernel(
    half, at, timestep, winner, latents, noise, feats, rows_y, rows_yc, rows_x, rows_xc, got_c,
    got_y, got_yc, got_x, got_xc, diag_0, diag_1, diag_c0, diag_c1, policy, reference, ref_y, ref_c,
    gap, near, near_x, far, far_x,
    rows_ref, both, clean, drawn, grad, sems,
):
    tok, width = feats.shape
    h = tok // 2
    pair, yh, yl, c, xh, xl, own = (at[i] for i in range(7))
    time = (timestep[pair].astype(f32) + 0.5) / STEPS
    sign = jnp.where(winner[pair] == xl, 1.0, -1.0).astype(f32)
    mine = pl.ds(pl.multiple_of(own * half, 128), half)
    count = [0]

    def start(source, target):
        copy = pltpu.make_async_copy(source, target, sems.at[count[0]])
        count[0] += 1
        copy.start()
        return copy

    def lanes(first, size=half):
        return pl.ds(first * half, size)

    def rows_of(k):
        return pl.ds(k * tok, tok)

    n_z, depth = policy.shape[0], policy.shape[2]
    weight_copies = [
        start(policy.at[z, y], both.at[pl.ds((y * n_z + z) * depth, depth), lanes(0)])
        for z in range(n_z)
        for y in range(2)
    ]
    block = reference.shape[0]
    for dy, dc, source in (
        (0, 0, reference.at[:, mine]),
        (0, 1, ref_c.at[:, lanes(0)]),
        (1, 0, ref_y.at[:, lanes(0)]),
        (1, 1, ref_c.at[:, lanes(1)]),
    ):
        place = ((yl ^ dy ^ yh) * 2 + (c ^ dc)) * block
        target = both.at[pl.ds(pl.multiple_of(place, block), block), lanes(1)]
        weight_copies.append(start(source, target))

    def piece(k, source, feats_at, beside, clean_at, drawn_at):
        copies = [
            start(source.at[:, lanes(feats_at, width)], rows_ref.at[rows_of(k)]),
            start(beside.at[:, lanes(clean_at)], clean.at[rows_of(k)]),
        ]
        if drawn_at is not None:
            copies.append(start(beside.at[:, lanes(drawn_at)], drawn.at[rows_of(k)]))
        return copies

    def halves(k, source):
        copies = []
        for i in range(2):
            part, rows = source[i], pl.ds(k * tok + i * h, h)
            copies.append(start(part.at[:, lanes(0, width)], rows_ref.at[rows]))
            copies.append(start(part.at[:, lanes(9 if k == 5 else 8)], clean.at[rows]))
        return copies

    chunks = [
        [
            start(feats, rows_ref.at[rows_of(0)]),
            start(latents.at[:, mine], clean.at[rows_of(0)]),
            start(noise.at[:, mine], drawn.at[rows_of(0)]),
        ]
        + piece(1, rows_y, 0, got_y, 0, 1),
        piece(2, got_c, 2, got_c, 0, 1) + piece(3, rows_yc, 0, got_yc, 2, 3),
        piece(4, rows_x, 0, got_x, 0, None) + halves(5, (diag_0, diag_1)),
        piece(6, rows_xc, 0, got_xc, 1, None) + halves(7, (diag_c0, diag_c1)),
    ]
    for copy in weight_copies:
        copy.wait()
    total = jnp.zeros((1, half), f32)
    for i, copies in enumerate(chunks):
        for copy in copies:
            copy.wait()
        rows = pl.ds(i * 2 * tok, 2 * tok)
        out = jnp.dot(rows_ref[rows, :], both[...], preferred_element_type=f32)
        start_rows = clean[rows, :].astype(f32)
        noise_rows = drawn[pl.ds((i % 2) * 2 * tok, 2 * tok), :].astype(f32)
        base = ((1.0 - time) * start_rows + time * noise_rows) - (noise_rows - start_rows)
        policy_diff = base + out[:, :half].astype(bf16).astype(f32)
        ref_diff = base + out[:, half:]
        signed = sign if i < 2 else -sign
        grad[rows, :] = (signed * policy_diff).astype(bf16)
        excess = policy_diff * policy_diff - ref_diff * ref_diff
        total = total + signed * jnp.sum(excess, axis=0, keepdims=True)
    gap[...] = jnp.broadcast_to(jnp.sum(total, axis=1, keepdims=True), gap.shape)

    per = depth // 2
    for y, same, other in ((1, far, far_x), (0, near, near_x)):
        for z in range(0, n_z, 2):
            part = lax.dot_general(
                rows_ref[:, pl.ds((y * n_z + z) * depth, 2 * depth)],
                grad[...],
                (((0,), (0,)), ((), ())),
                preferred_element_type=f32,
            ).astype(bf16)
            for k in range(2):
                low = part[2 * k * per : (2 * k + 1) * per]
                high = part[(2 * k + 1) * per : (2 * k + 2) * per]
                rows = pl.ds((z + k) * per, per)
                same[rows, :] = jnp.where(xh == 0, low, high)
                other[rows, :] = jnp.where(xh == 0, high, low)
    tail = pl.ds(n_z * per, 16)
    for out in (near, near_x, far, far_x):
        out[tail, :] = jnp.zeros((16, half), bf16)


def project(at, timestep, winner, half, *arrays):
    tok, width = arrays[2].shape
    policy = arrays[16]
    out_rows = policy.shape[0] * policy.shape[2] // 2 + 16
    small = pl.BlockSpec(memory_space=pltpu.SMEM)
    block = jax.ShapeDtypeStruct((out_rows, half), bf16)
    return pl.pallas_call(
        lambda *refs: project_kernel(half, *refs),
        in_specs=[small] * 3 + [pl.BlockSpec(memory_space=pl.ANY)] * len(arrays),
        out_specs=[pl.BlockSpec(memory_space=pltpu.VMEM)] * 5,
        out_shape=[jax.ShapeDtypeStruct((8, 128), f32)] + [block] * 4,
        scratch_shapes=[
            pltpu.VMEM((8 * tok, width), bf16),
            pltpu.VMEM((width, 2 * half), bf16),
            pltpu.VMEM((8 * tok, half), bf16),
            pltpu.VMEM((4 * tok, half), bf16),
            pltpu.VMEM((8 * tok, half), bf16),
            pltpu.SemaphoreType.DMA((48,)),
        ],
        compiler_params=pltpu.CompilerParams(vmem_limit_bytes=56 * 2**20),
        cost_estimate=pl.CostEstimate(
            flops=6 * 8 * tok * width * half, bytes_accessed=16 * 2**20, transcendentals=0
        ),
        name="project",
    )(at, timestep, winner, *arrays)


def stamp_kernel(scale, gap, gap_x, gap_y, gap_d, margin, terms):
    total = gap_x[...] + gap_y[...] + (gap_d[...] + gap[...])
    value = -0.5 * BETA * (total / scale)
    margin[...] = value
    value = value[:1, :1]
    first = value.astype(bf16).astype(f32)
    second = (value - first).astype(bf16).astype(f32)
    third = (value - first) - second
    row = lax.broadcasted_iota(jnp.int32, terms.shape, 0)
    rest = jnp.where(row == 2, third, 0.0)
    terms[...] = jnp.where(row == 0, first, jnp.where(row == 1, second, rest)).astype(bf16)


def stamp(scale, half, *gaps):
    return pl.pallas_call(
        lambda *refs: stamp_kernel(scale, *refs),
        out_shape=[
            jax.ShapeDtypeStruct(gaps[0].shape, f32),
            jax.ShapeDtypeStruct((16, half), bf16),
        ],
        name="stamp",
    )(*gaps)


def combine_kernel(factor, margin, near, got_x, got_y, got_d, out):
    size = out.shape[0]

    def weight(value):
        return (jax.nn.sigmoid(-value) * factor)[:1, :1]

    total = weight(margin[...]) * near[:size, :].astype(f32)
    for block in (got_x, got_y, got_d):
        terms = block[size : size + 16, :128].astype(f32)
        value = (terms[0:1] + terms[1:2]) + terms[2:3]
        total = total + weight(value) * block[:size, :].astype(f32)
    out[...] = total.astype(bf16)


def combine(factor, margin, *blocks):
    rows, half = blocks[0].shape
    return pl.pallas_call(
        lambda *refs: combine_kernel(factor, *refs),
        out_shape=jax.ShapeDtypeStruct((rows - 16, half), bf16),
        compiler_params=pltpu.CompilerParams(vmem_limit_bytes=24 * 2**20),
        name="combine",
    )(margin, *blocks)


def body(
    latents, noise, timestep, winner, norm_gain, reference_weight, policy_master, moment_first, moment_second
):
    tok, width = latents.shape
    yh, z, xh, xl, yl, c = (lax.axis_index(a) for a in AXES)
    half = policy_master.shape[1] // 2
    pair = (yh * SIZES[1] + z) * SIZES[2] + xh
    count_pairs = timestep.shape[0]
    scale = float(4 * tok * width)
    def columns(array, dx, dy, dc):
        block = ((yl ^ dy) * 2 + (c ^ dc)) * 2 + (xl ^ dx)
        return lax.dynamic_slice_in_dim(array, block * half, half, 1)

    policy_bf = policy_master.astype(bf16)
    own_w = lax.dynamic_slice_in_dim(policy_bf, xl * half, half, 1)
    other_w = flip(lax.dynamic_slice_in_dim(policy_bf, (1 - xl) * half, half, 1), "xl")
    blocks = [
        ((yl ^ dy) * 2 + (c ^ dc)) * 2 + (xl ^ dx)
        for dx, dy in ((0, 0), (0, 1), (1, 0), (1, 1))
        for dc in (0, 1)
    ]
    at = jnp.stack([pair, yh] + blocks[1:])
    feats, send, send_y, send_x, send_c = pack(at, timestep, latents, noise, norm_gain, half)
    own_w = ordered(xl, own_w, other_w)
    same_z = jnp.stack(
        [
            ordered(xh, own_w[None], after(flip(own_w, "xh"), feats)[None]),
            ordered(xh, flip(own_w, "yh")[None], flip(own_w, "yh", "xh")[None]),
        ]
    )[:, None]

    send, send_c, weight_in, _ = lax.optimization_barrier((send, send_c, reference_weight, same_z))
    rows_y, rows_x, got_c = flip(send, "yl"), flip(send, "xl"), flip(send_c, "c")

    ref_y = flip(
        jnp.concatenate([columns(weight_in, 0, 1, 0), columns(weight_in, 0, 1, 1)], 1), "yh", "yl"
    )
    send_y, send_x = after(send_y, rows_y, rows_x), after(send_x, rows_y, rows_x, ref_y)
    got_y, got_x = flip(send_y, "yl"), flip(send_x, "xl")

    n_z = SIZES[1]
    per_z = lax.all_gather(same_z.reshape(-1, half), "z").reshape(n_z, 2, -1, half)

    h = tok // 2
    diag = [flip(rows_y[:h], "xl"), flip(rows_x[h:], "yl")]
    ref_y = after(ref_y, *diag)
    ref_c = flip(jnp.concatenate([columns(weight_in, 0, 0, 1), ref_y[:, half:]], 1), "c")
    diag_c = [flip(part, "c") for part in diag]
    rows_yc, rows_xc = flip(rows_y, "c"), flip(rows_x, "c")
    got_yc, got_xc = flip(got_y, "c"), flip(got_x, "c")

    places = jnp.stack([pair, yh, yl, c, xh, xl, blocks[0]])
    gap, near, near_x, far, far_x = project(
        places, timestep, winner, half, latents, noise, feats, rows_y, rows_yc, rows_x, rows_xc,
        got_c, got_y, got_yc, got_x, got_xc, *diag, *diag_c, per_z, reference_weight, ref_y, ref_c,
    )

    gap = gap + flip(gap, "c")
    margin, terms = stamp(
        scale, half, gap, flip(gap, "xl"), flip(gap, "yl"), flip(gap, "xl", "yl")
    )
    size = near.shape[0] - 16

    def with_margin(block):
        return lax.dynamic_update_slice(block, terms, (size, 0))

    got_x = flip(with_margin(near_x), "xh")
    got_y = flip(with_margin(far), "yh")
    got_d = flip(with_margin(far_x), "yh", "xh")
    loss = jax.nn.softplus(-margin[0, 0])
    for step in (1, 2, 4):
        loss = loss + lax.ppermute(loss, "z", [(i, i ^ step) for i in range(n_z)])
    factor = BETA / (2.0 * count_pairs) * (2.0 / scale)
    summed = combine(factor, after(margin, loss), near, got_x, got_y, got_d)
    loss = after(loss, summed)
    loss = (loss + flip(loss, "xh")) + (flip(loss, "yh") + flip(loss, "yh", "xh"))
    loss = loss / count_pairs
    rows = policy_master.shape[0]
    blocks = lax.all_to_all(
        summed.reshape(-1, rows, half), ("z", "xl"), split_axis=0, concat_axis=0, tiled=True
    )
    blocks = blocks.reshape(SIZES[1], 2, rows, half).astype(f32).sum(axis=0)
    gradient = jnp.concatenate([blocks[0], blocks[1]], axis=1)
    return adam_update(policy_master, moment_first, moment_second, gradient) + (loss,)


def solution(mesh):
    fine = Mesh(mesh.devices.reshape(SIZES), AXES)
    fsdp, tp = AXES[:4], AXES[4:]
    return jax.shard_map(
        body,
        mesh=fine,
        in_specs=(P(AXES, None), P(AXES, None), P(), P(), P(), P(tp, None))
        + (P(fsdp, tp),) * 3,
        out_specs=(P(fsdp, tp), P(fsdp, tp), P(fsdp, tp), P()),
        check_vma=False,
    )
```
